32 devices in a mesh: dp: 4 (over y, x), expert: 4 (over z), tensor: 2 (over core).
Axes of the slice: x: 2, y: 2, z: 4, core: 2. Of those that a mesh axis runs over, the one named last changes fastest.
Arguments:
- out_grad: bfloat16 [2048, 3584], P(('dp', 'expert'), 'tensor'), may hold values from -6 to 6
- routing: int32 [2048, 8], P(('dp', 'expert')), may hold values from 0 to 15, all different within a row; in each aligned block of 128 rows (0 to 127, 128 to 255, ...) at most 128 rows name the same one
- route_probs: float32 [2048, 8], P(('dp', 'expert')), may hold values from 0.05 to 1
- w_down: bfloat16 [4, 3584, 1024], P('expert', 'dp', 'tensor'), may hold values from -0.1875 to 0.1875
- saved_gate: bfloat16 [8192, 1024], P(('dp', 'expert'), 'tensor'), may hold values from -8 to 8
- saved_up: bfloat16 [8192, 1024], P(('dp', 'expert'), 'tensor'), may hold values from -6 to 6
Outputs:
- weight_grad: bfloat16 [4, 3584, 1024], P('expert', 'dp', 'tensor')
- grad_gate: bfloat16 [8192, 1024], P(('dp', 'expert'), 'tensor')
- grad_up: bfloat16 [8192, 1024], P(('dp', 'expert'), 'tensor')
- grad_amax: float32 [4, 4], P('dp', 'expert')
The draws below stay inside these ranges and needn't reach their ends.
Inputs may be any that keep to these rules, and one draw needn't show every extreme that they name: `routing`: each row names 8 different experts; in the rows of one device no expert is named more than 128 times.
All inputs are finite; a program needn't handle non-finite values. Where the reference program divides by a largest or mean magnitude, that divisor is 1e-20 or more.
Results may differ from the reference program's by a relative error of at most 0.009.
Values may be sent and summed in bfloat16 or wider, within the bound.
No kernel may reach another device: no remote copies, remote signals or barrier semaphores. Data moves between devices by JAX's collectives and lax.ppermute only.
A program may use at most 64 MiB of HBM per device.

```python
import math
import jax
import jax.numpy as jnp
import numpy as np
from jax import lax

D = 3584
F = 1024
TOP = 8
TOK_DEV = 128
EXPERTS = 16
CAP = 128
SLOTS = 512
TOKENS = 2048
N_DP = 4
N_EXPERT = 4


def block_scale(key, dims, shards, smallest, largest):
    level = 1.0
    for axis_at, blocks in shards:
        heights = jax.random.uniform(jax.random.fold_in(jax.random.fold_in(key, 6), axis_at), (blocks,), jnp.float32, smallest / len(shards), largest / len(shards))
        level = level * jnp.repeat(jnp.exp(heights), dims[axis_at] // blocks).reshape((-1,) + (1,) * (len(dims) - 1 - axis_at))
    return level


def routed_block(own_key, own, number, rows, count, top, most, skew):
    ranking = jax.random.permutation(own_key, count)
    heavy_load, usual = portions_of(count, rows * top, most, skew, True), portions_of(count, rows * top, most, skew, False)
    places = jnp.arange(count)

    def named(lengths, offset_by):
        used = int((lengths > 0).sum())
        fixed = max(1, used // 4)
        moved = fixed + (places - fixed + offset_by * (used - fixed)) % max(1, count - fixed)
        return jnp.zeros((count,), jnp.int32).at[ranking[jnp.where(places < fixed, places, moved)]].set(jnp.asarray(lengths, jnp.int32))

    lengths = jnp.where(number % 4 == 0, named(heavy_load, number // 4), named(usual, number - number // 4 - 1))
    mixed = jax.random.permutation(jax.random.fold_in(own, 3), count)
    donor, receiver = mixed[0:count // 2 * 2:2], mixed[1:count // 2 * 2:2]
    slack = jnp.minimum(lengths[donor] - 1, most - lengths[receiver]) // 2
    slack = jnp.where((donor == ranking[0]) | (receiver == ranking[0]) | (lengths[receiver] == 0), 0, jnp.maximum(slack, 0))
    moved = jax.random.randint(jax.random.fold_in(own, 4), (count // 2,), 0, 1 << 20) % (slack + 1)
    lengths = lengths.at[donor].add(-moved).at[receiver].add(moved)
    items = jnp.searchsorted(jnp.cumsum(lengths), jnp.arange(rows * top), side="right").astype(jnp.int32)
    table = items.reshape(top, rows).T
    table = table[jax.random.permutation(jax.random.fold_in(own, 1), rows)]
    offset_by = jax.random.randint(jax.random.fold_in(own, 2), (rows, 1), 0, top)
    return jnp.take_along_axis(table, (jnp.arange(top)[None, :] + offset_by) % top, axis=1)


def portions_of(amount, total, limit, lean, full):
    loads = [(1 << 20) // math.isqrt(rank ** lean) + 1 for rank in range(1, amount + 1)]
    largest = limit if full else min(limit, max(-(-total // amount), total * loads[0] // sum(loads)))
    least = 1 if total - largest >= amount - 1 else 0
    given, surplus = [largest] + [least] * (amount - 1), total - largest - least * (amount - 1)
    while surplus > 0:
        candidates = [i for i in range(1, amount) if given[i] < largest] or [i for i in range(1, amount) if given[i] < limit]
        pool, budget = sum([loads[i] for i in candidates]), surplus
        for i in candidates:
            more = min(limit - given[i], max(1, budget * loads[i] // pool), surplus)
            given[i] = given[i] + more
            surplus = surplus - more
    return np.array(given)


def gaussian(own_key, dims, spread, reach, cuts=(), kind=jnp.bfloat16):
    entries = jax.random.normal(own_key, dims, jnp.float32) * spread
    if len(cuts) > 0:
        entries = block_scale(own_key, dims, cuts, -0.22, 0.18) * entries
    return jnp.clip(entries, min=-reach, max=reach).astype(kind)


def setup_inputs(seed: int = 0) -> dict:
    splits = jax.random.split(jax.random.key(seed), 7)
    out_grad = gaussian(splits[0], (TOKENS, D), 1.0, 6.0, ((0, 16), (1, 2)))
    routing_keys = jax.random.split(jax.random.fold_in(splits[1], 1), TOKENS // TOK_DEV)
    routing_turns = jax.random.permutation(jax.random.fold_in(splits[1], 3), TOKENS // TOK_DEV)
    routing = jax.vmap(lambda own, number: routed_block(jax.random.fold_in(splits[1], 2), own, number, TOK_DEV, EXPERTS, TOP, CAP, 2))(routing_keys, routing_turns).reshape((TOKENS, TOP))
    route_probs = jnp.clip(jnp.exp(math.log(1.0) - 2.9957323 * jax.random.uniform(splits[2], (TOKENS, TOP), jnp.float32) ** block_scale(splits[2], (TOKENS, TOP), ((0, 16),), -0.2, 0.2)), 0.05, 1.0)
    w_down = gaussian(splits[3], (N_EXPERT, D, F), F ** -0.5, 0.1875, ((0, 4), (1, 4), (2, 2)))
    saved_gate = gaussian(splits[4], (N_DP * N_EXPERT * SLOTS, F), 2.0, 8.0, ((0, 16), (1, 2)))
    saved_up = gaussian(splits[5], (N_DP * N_EXPERT * SLOTS, F), 1.0, 6.0, ((0, 16), (1, 2)))
    return {"out_grad": out_grad, "routing": routing, "route_probs": route_probs, "w_down": w_down, "saved_gate": saved_gate, "saved_up": saved_up}


epsilon = 1e-6


def reference(out_grad, routing, route_probs, w_down, saved_gate, saved_up):
    owners = N_EXPERT
    blocks = N_DP * N_EXPERT
    slot_count = N_EXPERT * CAP
    total = N_DP * N_EXPERT * slot_count
    matches = routing[:, :, None] == jnp.arange(owners, dtype=jnp.int32)[None, None, :]
    is_routed = jnp.any(matches, axis=1).astype(jnp.int32)
    scaling = jnp.sum(jnp.where(matches, route_probs[:, :, None], 0.0), axis=1)
    per_block = is_routed.reshape(blocks, TOK_DEV, owners)
    slot_rank = jnp.cumsum(per_block, axis=1) - per_block
    block_ids = jnp.arange(blocks, dtype=jnp.int32)[:, None, None]
    group_ids = block_ids // owners
    source_ids = block_ids % owners
    expert_ids = jnp.arange(owners, dtype=jnp.int32)[None, None, :]
    target = ((group_ids * owners + expert_ids) * owners + source_ids) * CAP + slot_rank
    target = jnp.where(per_block == 1, target, total).reshape(-1).astype(jnp.int32)
    token_ids = jnp.broadcast_to(jnp.arange(blocks * TOK_DEV, dtype=jnp.int32).reshape(blocks, TOK_DEV, 1), per_block.shape).reshape(-1)
    slot_token = jnp.zeros((total,), jnp.int32).at[target].set(token_ids, mode="drop")
    slot_scale = jnp.zeros((total,), scaling.dtype).at[target].set(scaling.reshape(-1), mode="drop")

    def per_expert(expert_id):
        weight = lax.dynamic_index_in_dim(w_down, expert_id, 0, keepdims=False)
        summed = jnp.zeros((D, F), jnp.float32)
        gates = []
        ups = []
        maxima = []
        for group_id in range(N_DP):
            start = ((group_id * owners + expert_id) * slot_count).astype(jnp.int32)
            tokens = lax.dynamic_slice_in_dim(slot_token, start, slot_count)
            scales = lax.dynamic_slice_in_dim(slot_scale, start, slot_count)
            slot_rows = (jnp.take(out_grad, tokens, axis=0).astype(jnp.float32) * scales[:, None]).astype(jnp.bfloat16)
            grad_hidden = jnp.dot(slot_rows, weight, preferred_element_type=jnp.float32)
            grad_amax = jnp.max(jnp.abs(grad_hidden))
            quantized = lax.optimization_barrier((grad_hidden / (grad_amax + epsilon)).astype(jnp.bfloat16)).astype(jnp.float32)
            gate_pre = lax.dynamic_slice_in_dim(saved_gate, start, slot_count).astype(jnp.float32)
            up_pre = lax.dynamic_slice_in_dim(saved_up, start, slot_count).astype(jnp.float32)
            sigmoid_gate = jax.nn.sigmoid(gate_pre)
            silu_gate = gate_pre * sigmoid_gate
            gates.append((quantized * up_pre * sigmoid_gate * (1.0 + gate_pre * (1.0 - sigmoid_gate))).astype(jnp.bfloat16))
            ups.append((quantized * silu_gate).astype(jnp.bfloat16))
            activation = (silu_gate * up_pre).astype(jnp.bfloat16)
            partial_value = lax.dot_general(slot_rows, activation, (((0,), (0,)), ((), ())), preferred_element_type=jnp.float32)
            summed = summed + lax.optimization_barrier(partial_value.astype(jnp.bfloat16)).astype(jnp.float32)
            maxima.append(grad_amax)
        return summed.astype(jnp.bfloat16), jnp.stack(gates), jnp.stack(ups), jnp.stack(maxima)

    grads, gates, ups, maxima = lax.map(per_expert, jnp.arange(owners, dtype=jnp.int32))
    grad_gate = jnp.transpose(gates, (1, 0, 2, 3)).reshape(total, F)
    grad_up = jnp.transpose(ups, (1, 0, 2, 3)).reshape(total, F)
    return grads, grad_gate, grad_up, jnp.transpose(maxima)
```

```python
import jax
import jax.numpy as jnp
from jax import lax
from jax.sharding import PartitionSpec as P

epsilon = 1e-06


def ranks(flags):
    rows = flags.shape[0]
    at = lax.broadcasted_iota(jnp.int32, (rows, rows), 0)
    before = lax.broadcasted_iota(jnp.int32, (rows, rows), 1) < at
    counts = jnp.dot(
        before.astype(jnp.bfloat16), flags.astype(jnp.bfloat16), preferred_element_type=jnp.float32
    )
    return counts.astype(jnp.int32)


def route(routing, route_probs, owners):
    matches = routing[:, :, None] == jnp.arange(owners, dtype=jnp.int32)[None, None, :]
    is_routed = jnp.any(matches, axis=1)
    scaling = jnp.sum(jnp.where(matches, route_probs[:, :, None], 0.0), axis=1)
    return is_routed, scaling, ranks(is_routed)


def by_slots(out_grad, routing, route_probs, w_down, saved_gate, saved_up):
    owners = lax.axis_size("expert")
    slot_count = saved_gate.shape[0]
    capacity = slot_count // owners
    is_routed, scaling, slot_rank = route(routing, route_probs, owners)
    picked = is_routed[:, :, None] & (
        slot_rank[:, :, None] == jnp.arange(capacity, dtype=jnp.int32)[None, None, :]
    )
    token_ids = jnp.arange(routing.shape[0], dtype=jnp.int32)[:, None, None]
    slot_token = jnp.sum(jnp.where(picked, token_ids, 0), axis=0)
    slot_scale = jnp.sum(jnp.where(picked, scaling[:, :, None], 0.0), axis=0)
    picked_rows = jnp.take(out_grad, slot_token, axis=0)
    arrived = lax.all_to_all(
        (picked_rows.astype(jnp.float32) * slot_scale[:, :, None]).astype(jnp.bfloat16),
        "expert",
        split_axis=0,
        concat_axis=0,
        tiled=True,
    )
    slot_rows = lax.all_gather(
        arrived.reshape(slot_count, out_grad.shape[1]), "tensor", axis=1, tiled=True
    )
    grad_hidden = jnp.dot(
        slot_rows,
        lax.all_gather(w_down, "dp", axis=1, tiled=True)[0],
        preferred_element_type=jnp.float32,
    )
    gate_pre = saved_gate.astype(jnp.float32)
    up_pre = saved_up.astype(jnp.float32)
    sigmoid_gate = jax.nn.sigmoid(gate_pre)
    silu_gate = gate_pre * sigmoid_gate
    activation = (silu_gate * up_pre).astype(jnp.bfloat16)
    grad_amax = lax.pmax(jnp.max(jnp.abs(grad_hidden)), "tensor")
    weight_sum = lax.psum_scatter(
        lax.dot_general(
            slot_rows, activation, (((0,), (0,)), ((), ())), preferred_element_type=jnp.float32
        ).astype(jnp.bfloat16),
        "dp",
        scatter_dimension=0,
        tiled=True,
    )
    quantized = (grad_hidden / (grad_amax + epsilon)).astype(jnp.bfloat16).astype(jnp.float32)
    grad_gate = (
        quantized * up_pre * sigmoid_gate * (1.0 + gate_pre * (1.0 - sigmoid_gate))
    ).astype(jnp.bfloat16)
    grad_up = (quantized * silu_gate).astype(jnp.bfloat16)
    return (weight_sum.reshape(w_down.shape), grad_gate, grad_up, grad_amax.reshape(1, 1))


def by_tokens(out_grad, routing, route_probs, w_down, saved_gate, saved_up):
    n_dp, owners, cores = (lax.axis_size(a) for a in ("dp", "expert", "tensor"))
    p, e, t = (lax.axis_index(a) for a in ("dp", "expert", "tensor"))
    tokens = routing.shape[0]
    depth, hidden = w_down.shape[1:]
    slot_count = saved_gate.shape[0]
    capacity = slot_count // owners
    per_core = n_dp // cores
    weight = w_down[0]

    def turn(k):
        return [(s, (s + k) % owners) for s in range(owners)]

    is_routed, scaling, slot_rank = route(routing, route_probs, owners)
    slot_of = jnp.where(is_routed, e * capacity + slot_rank, -1).astype(jnp.float32)
    tables = jnp.stack([slot_of.T, scaling.T], axis=1)
    got = [
        lax.ppermute(lax.dynamic_index_in_dim(tables, (e + k) % owners, 0, keepdims=False), "expert", turn(k))
        if k
        else lax.dynamic_index_in_dim(tables, e, 0, keepdims=False)
        for k in range(owners)
    ]
    got = jnp.stack(got, axis=1)

    chunks = CHUNKS
    bounds, cuts = 0, []
    for i in range(chunks):
        cuts.append((i * tokens // chunks, (i + 1) * tokens // chunks))
    order = jnp.concatenate([got[:, :, a:b].reshape(2, -1) for a, b in cuts], axis=1)
    slot_id, scale = order[0].astype(jnp.int32), order[1]

    def to_dp(j):
        pairs = []
        for src in range(n_dp):
            for core in range(cores):
                q = core * per_core + (src % per_core + j) % per_core
                u = (src // per_core - core) % cores
                pairs.append((src * cores + core, q * cores + u))
        return pairs

    def to_group(u_of, j):
        pairs = []
        for q in range(n_dp):
            for core in range(cores):
                d1 = u_of(core)
                dest = ((q // per_core + d1) % cores) * per_core + (q % per_core - j) % per_core
                pairs.append((q * cores + core, dest * cores + core))
        return pairs

    gate_pre = saved_gate.astype(jnp.float32)
    up_pre = saved_up.astype(jnp.float32)
    sigmoid_gate = jax.nn.sigmoid(gate_pre)
    silu_gate = gate_pre * sigmoid_gate
    activation = (silu_gate * up_pre).astype(jnp.bfloat16)
    for_gate = up_pre * sigmoid_gate * (1.0 + gate_pre * (1.0 - sigmoid_gate))
    pick = (lax.broadcasted_iota(jnp.int32, (slot_count, slot_id.shape[0]), 0) == slot_id[None, :]).astype(
        jnp.bfloat16
    )
    in_tokens = lax.dot_general(
        pick, activation, (((0,), (0,)), ((), ())), preferred_element_type=jnp.float32
    )
    in_tokens = (in_tokens * scale[:, None]).astype(jnp.bfloat16)

    def from_group(u_of, j):
        return [(b, a) for a, b in to_group(u_of, j)]

    others = []
    for x in range(1, cores + 1):
        for j in range(per_core):
            u_of = lambda core, x=x: (core + x) % cores
            others.append(lax.ppermute(in_tokens, ("dp", "tensor"), from_group(u_of, j)))

    mine_x, other_x, partial = [], [], []
    for a, b in cuts:
        first = []
        for j in range(per_core):
            block = lax.dynamic_slice(
                out_grad, (jnp.int32(a), (p % per_core + j) % per_core * depth), (b - a, depth)
            )
            first.append(lax.ppermute(block, ("dp", "tensor"), to_dp(j)))
        first = jnp.stack(first)
        rows = jnp.stack([first] + [lax.ppermute(first, "expert", turn(k)) for k in range(1, owners)], axis=1)
        rows = rows.reshape(per_core, -1, depth)
        mine_x.append(rows)
        swapped = [
            lax.ppermute(rows, "tensor", [(c, (c - x) % cores) for c in range(cores)]) for x in range(1, cores)
        ]
        other_x.append(swapped)
        sums = None
        for x in range(cores):
            held = rows if x == 0 else swapped[x - 1]
            for j in range(per_core):
                piece = jnp.dot(held[j], weight, preferred_element_type=jnp.float32)
                piece = piece.astype(jnp.bfloat16)
                u_of = lambda core, x=x: (core + x) % cores
                piece = lax.ppermute(piece, ("dp", "tensor"), to_group(u_of, j)).astype(jnp.float32)
                sums = piece if sums is None else sums + piece
        partial.append(sums)

    total = jnp.concatenate(partial, axis=0) * scale[:, None]
    amax = jnp.max(jnp.abs(total)).reshape(1, 1)
    grad_amax = lax.pmax(amax, "tensor")
    high = total.astype(jnp.bfloat16)
    low = (total - high.astype(jnp.float32)).astype(jnp.bfloat16)
    grad_hidden = jnp.dot(pick, high, preferred_element_type=jnp.float32) + jnp.dot(
        pick, low, preferred_element_type=jnp.float32
    )
    quantized = (grad_hidden / (grad_amax + epsilon)).astype(jnp.bfloat16).astype(jnp.float32)
    grad_gate = (quantized * for_gate).astype(jnp.bfloat16)
    grad_up = (quantized * silu_gate).astype(jnp.bfloat16)

    weight_sum = 0.0
    for x in range(cores):
        for j in range(per_core):
            acts = others[(x - 1) % cores * per_core + j]
            held = jnp.concatenate(
                [(mine_x[i] if x == 0 else other_x[i][x - 1])[j] for i in range(chunks)], axis=0
            )
            weight_sum += lax.dot_general(
                held, acts, (((0,), (0,)), ((), ())), preferred_element_type=jnp.float32
            )
    return (weight_sum.astype(jnp.bfloat16).reshape(w_down.shape), grad_gate, grad_up, grad_amax)


CHUNKS = 2


def solution(mesh):
    placed = (
        P(("dp", "expert"), "tensor"),
        P(("dp", "expert"), None),
        P(("dp", "expert"), None),
        P("expert", "dp", "tensor"),
        P(("dp", "expert"), "tensor"),
        P(("dp", "expert"), "tensor"),
    )

    def body(out_grad, routing, route_probs, w_down, saved_gate, saved_up):
        capacity = saved_gate.shape[0] // mesh.shape["expert"]
        whole = capacity >= routing.shape[0] and mesh.shape["dp"] % mesh.shape["tensor"] == 0
        return (by_tokens if whole else by_slots)(
            out_grad, routing, route_probs, w_down, saved_gate, saved_up
        )

    return jax.shard_map(
        body,
        mesh=mesh,
        in_specs=placed,
        out_specs=(
            P("expert", "dp", "tensor"),
            P(("dp", "expert"), "tensor"),
            P(("dp", "expert"), "tensor"),
            P("dp", "expert"),
        ),
        check_vma=False,
    )
```

```python
import jax
import jax.numpy as jnp
from jax import lax
from jax.sharding import PartitionSpec as P

epsilon = 1e-06


def ranks(flags):
    rows = flags.shape[0]
    at = lax.broadcasted_iota(jnp.int32, (rows, rows), 0)
    before = lax.broadcasted_iota(jnp.int32, (rows, rows), 1) < at
    counts = jnp.dot(
        before.astype(jnp.bfloat16), flags.astype(jnp.bfloat16), preferred_element_type=jnp.float32
    )
    return counts.astype(jnp.int32)


def route(routing, route_probs, owners):
    matches = routing[:, :, None] == jnp.arange(owners, dtype=jnp.int32)[None, None, :]
    is_routed = jnp.any(matches, axis=1)
    scaling = jnp.sum(jnp.where(matches, route_probs[:, :, None], 0.0), axis=1)
    return is_routed, scaling, ranks(is_routed)


def by_slots(out_grad, routing, route_probs, w_down, saved_gate, saved_up):
    owners = lax.axis_size("expert")
    slot_count = saved_gate.shape[0]
    capacity = slot_count // owners
    is_routed, scaling, slot_rank = route(routing, route_probs, owners)
    picked = is_routed[:, :, None] & (
        slot_rank[:, :, None] == jnp.arange(capacity, dtype=jnp.int32)[None, None, :]
    )
    token_ids = jnp.arange(routing.shape[0], dtype=jnp.int32)[:, None, None]
    slot_token = jnp.sum(jnp.where(picked, token_ids, 0), axis=0)
    slot_scale = jnp.sum(jnp.where(picked, scaling[:, :, None], 0.0), axis=0)
    picked_rows = jnp.take(out_grad, slot_token, axis=0)
    arrived = lax.all_to_all(
        (picked_rows.astype(jnp.float32) * slot_scale[:, :, None]).astype(jnp.bfloat16),
        "expert",
        split_axis=0,
        concat_axis=0,
        tiled=True,
    )
    slot_rows = lax.all_gather(
        arrived.reshape(slot_count, out_grad.shape[1]), "tensor", axis=1, tiled=True
    )
    grad_hidden = jnp.dot(
        slot_rows,
        lax.all_gather(w_down, "dp", axis=1, tiled=True)[0],
        preferred_element_type=jnp.float32,
    )
    gate_pre = saved_gate.astype(jnp.float32)
    up_pre = saved_up.astype(jnp.float32)
    sigmoid_gate = jax.nn.sigmoid(gate_pre)
    silu_gate = gate_pre * sigmoid_gate
    activation = (silu_gate * up_pre).astype(jnp.bfloat16)
    grad_amax = lax.pmax(jnp.max(jnp.abs(grad_hidden)), "tensor")
    weight_sum = lax.psum_scatter(
        lax.dot_general(
            slot_rows, activation, (((0,), (0,)), ((), ())), preferred_element_type=jnp.float32
        ).astype(jnp.bfloat16),
        "dp",
        scatter_dimension=0,
        tiled=True,
    )
    quantized = (grad_hidden / (grad_amax + epsilon)).astype(jnp.bfloat16).astype(jnp.float32)
    grad_gate = (
        quantized * up_pre * sigmoid_gate * (1.0 + gate_pre * (1.0 - sigmoid_gate))
    ).astype(jnp.bfloat16)
    grad_up = (quantized * silu_gate).astype(jnp.bfloat16)
    return (weight_sum.reshape(w_down.shape), grad_gate, grad_up, grad_amax.reshape(1, 1))


def by_tokens(out_grad, routing, route_probs, w_down, saved_gate, saved_up):
    n_dp, owners, cores = (lax.axis_size(a) for a in ("dp", "expert", "tensor"))
    p, e, t = (lax.axis_index(a) for a in ("dp", "expert", "tensor"))
    tokens = routing.shape[0]
    depth, hidden = w_down.shape[1:]
    slot_count = saved_gate.shape[0]
    capacity = slot_count // owners
    part = tokens // cores
    weight = w_down[0]

    def turn(k):
        return [(s, (s + k) % owners) for s in range(owners)]

    def over_dp(x, d):
        return lax.ppermute(x, "dp", [(q, q ^ d) for q in range(n_dp)])

    def swap(x):
        return lax.ppermute(x, "tensor", [(c, 1 - c) for c in range(cores)])

    keep = lax.dynamic_slice_in_dim(out_grad, t * part, part, 0)
    give = lax.dynamic_slice_in_dim(out_grad, (1 - t) * part, part, 0)
    came = swap(give)
    share = jnp.where(t == 0, jnp.concatenate([keep, came], axis=1), jnp.concatenate([came, keep], axis=1))
    blocks = [lax.dynamic_slice(share, (jnp.int32(0), (p ^ d) * depth), (part, depth)) for d in range(n_dp)]
    blocks = [over_dp(x, d) if d else x for d, x in enumerate(blocks)]

    is_routed, scaling, slot_rank = route(routing, route_probs, owners)
    slot_of = jnp.where(is_routed, e * capacity + slot_rank, -1).astype(jnp.float32)
    tables = jnp.stack([slot_of.T, scaling.T], axis=1)

    even = e % 2 == 0
    reach = jnp.where(even, owners - 1 - e, e)
    pairs_a = [(s, s ^ 1) for s in range(owners)]
    pairs_b = [(s, ((s + 1) ^ 1) - 1) for s in range(1, owners - 1)]

    def gather_line(x):
        from_a, from_b = [], []
        for step in range(owners - 1):
            a = lax.ppermute(x if step == 0 else from_b[step - 1], "expert", pairs_a)
            if step < owners - 2:
                from_b.append(lax.ppermute(x if step == 0 else from_a[step - 1], "expert", pairs_b))
            from_a.append(a)
        out = [x]
        for k in range(1, owners):
            got = from_a[k - 1]
            for a in range(1, k, 2):
                got = jnp.where(reach == a, from_b[k - a - 1], got)
            out.append(got)
        return out

    def source(k):
        way = jnp.where(even, 1, -1)
        return jnp.where(k <= reach, e + way * k, e - way * (k - reach))

    table_of = [lax.dynamic_index_in_dim(tables, e, 0, keepdims=False)]
    by_turn = [table_of[0]] + [
        lax.ppermute(lax.dynamic_index_in_dim(tables, (e + k) % owners, 0, keepdims=False), "expert", turn(k))
        for k in range(1, owners)
    ]
    by_turn = jnp.stack(by_turn)
    got = jnp.stack([by_turn[(e - source(k)) % owners] for k in range(owners)])
    got = got.reshape(owners, 2, cores, part)
    got = jnp.where(t == 0, got, got[:, :, ::-1])
    got = got.transpose(1, 0, 2, 3).reshape(2, -1)
    slot_id, scale = got[0].astype(jnp.int32), got[1]

    gate_pre = saved_gate.astype(jnp.float32)
    up_pre = saved_up.astype(jnp.float32)
    sigmoid_gate = jax.nn.sigmoid(gate_pre)
    silu_gate = gate_pre * sigmoid_gate
    activation = (silu_gate * up_pre).astype(jnp.bfloat16)
    for_gate = up_pre * sigmoid_gate * (1.0 + gate_pre * (1.0 - sigmoid_gate))
    pick = (lax.broadcasted_iota(jnp.int32, (slot_count, slot_id.shape[0]), 0) == slot_id[None, :]).astype(
        jnp.bfloat16
    )
    in_tokens = lax.dot_general(
        pick, activation, (((0,), (0,)), ((), ())), preferred_element_type=jnp.float32
    )
    in_tokens = (in_tokens * scale[:, None]).astype(jnp.bfloat16)
    acts = {0: in_tokens}
    for d in range(1, n_dp):
        if d.bit_count() == 1:
            acts[d] = over_dp(in_tokens, d)
    for d in range(1, n_dp):
        if d.bit_count() == 2:
            low = d & -d
            half = in_tokens.shape[0] // 2
            acts[d] = jnp.concatenate(
                [over_dp(acts[d - low][:half], low), over_dp(acts[low][half:], d - low)], axis=0
            )

    lines = [gather_line(jnp.stack(blocks[d : d + n_dp // 2])) for d in (0, n_dp // 2)]
    groups = [(0, 2)] + [(k, k + 1) for k in range(2, owners)]
    held, sums = [], []
    for a, b in groups:
        mine = jnp.concatenate([jnp.stack(line[a:b], axis=1) for line in lines])
        other = swap(mine)
        rows = jnp.stack([mine, other], axis=2).reshape(n_dp, -1, depth)
        held.append(rows)
        total = jnp.dot(rows[0], weight, preferred_element_type=jnp.float32)
        for d in range(1, n_dp):
            piece = jnp.dot(rows[d], weight, preferred_element_type=jnp.float32).astype(jnp.bfloat16)
            total += over_dp(piece, d).astype(jnp.float32)
        sums.append(total)

    total = jnp.concatenate(sums, axis=0) * scale[:, None]
    amax = jnp.max(jnp.abs(total)).reshape(1, 1)
    grad_amax = jnp.maximum(amax, swap(amax))
    high = lax.reduce_precision(total, 8, 7)
    low = (total - high).astype(jnp.bfloat16)
    grad_hidden = jnp.dot(pick, high.astype(jnp.bfloat16), preferred_element_type=jnp.float32) + jnp.dot(
        pick, low, preferred_element_type=jnp.float32
    )
    quantized = (grad_hidden / (grad_amax + epsilon)).astype(jnp.bfloat16).astype(jnp.float32)
    grad_gate = (quantized * for_gate).astype(jnp.bfloat16)
    grad_up = (quantized * silu_gate).astype(jnp.bfloat16)

    weight_sum = 0.0
    for d in range(n_dp):
        rows = jnp.concatenate([rows[d] for rows in held], axis=0)
        weight_sum += lax.dot_general(
            rows, acts[d], (((0,), (0,)), ((), ())), preferred_element_type=jnp.float32
        )
    return (weight_sum.astype(jnp.bfloat16).reshape(w_down.shape), grad_gate, grad_up, grad_amax)


def solution(mesh):
    placed = (
        P(("dp", "expert"), "tensor"),
        P(("dp", "expert"), None),
        P(("dp", "expert"), None),
        P("expert", "dp", "tensor"),
        P(("dp", "expert"), "tensor"),
        P(("dp", "expert"), "tensor"),
    )

    def body(out_grad, routing, route_probs, w_down, saved_gate, saved_up):
        capacity = saved_gate.shape[0] // mesh.shape["expert"]
        n_dp, owners, cores = (mesh.shape[a] for a in ("dp", "expert", "tensor"))
        whole = capacity >= routing.shape[0] and cores == 2 and owners % 2 == 0 and n_dp.bit_count() == 1 and n_dp >= cores
        return (by_tokens if whole else by_slots)(
            out_grad, routing, route_probs, w_down, saved_gate, saved_up
        )

    return jax.shard_map(
        body,
        mesh=mesh,
        in_specs=placed,
        out_specs=(
            P("expert", "dp", "tensor"),
            P(("dp", "expert"), "tensor"),
            P(("dp", "expert"), "tensor"),
            P("dp", "expert"),
        ),
        check_vma=False,
    )
```
